256 devices in a mesh: hist: 32 (over x_hi, z, core), user: 8 (over x_lo, y).
Axes of the slice: x: 4 (x_hi: 2, x_lo: 2; x = x_hi * 2 + x_lo), y: 4, z: 8, core: 2. Of those that a mesh axis runs over, the one named last changes fastest.
Arguments:
- candidate_proj: bfloat16 [8, 2048, 4096], P('user', 'hist'), may hold values from -6 to 6
- history_cache: bfloat16 [32, 128, 512, 256], P('hist', 'user'), may hold values from -6 to 6
- request_owner: int32 [8, 512, 1], P('user', 'hist'), may hold values from 0 to 7; in each aligned block of 16 rows (0 to 15, 16 to 31, ..., all dimensions but the last counted through in order) at most 3 rows name the same one
- request_page: int32 [8, 512], P('user', 'hist'), may hold values from 0 to 15
- history_length: int32 [8], P('user'), may hold values from 1 to 32768, 131080 in all
- candidate_count: int32 [8], P('user'), may hold values from 1 to 2048, 12296 in all
- block_mask: int32 [8, 32, 64], P('user'), may hold values 0 or 1
- norm_gain: float32 [1024], replicated, may hold values from 0.25 to 1.75
- w_out: bfloat16 [1024, 1024], replicated, may hold values from -0.1875 to 0.1875
Outputs:
- candidate_out: bfloat16 [8, 2048, 1024], P('user', 'hist')
The draws below stay inside these ranges and needn't reach their ends.
Inputs may be any that keep to these rules, and one draw needn't show every extreme that they name: `request_owner`: among the 16 rows of one device, at most 3 name the same owner. `history_length`: the longest history has 32768 events. `candidate_count`: the largest count is 2048.
All inputs are finite; a program needn't handle non-finite values. No bound on the sum of `history_length` or of `candidate_count` or of `block_mask` on one device may be relied on, other than what follows from the above.
Results may differ from the reference program's by a relative error of at most 0.022.
Values may be sent and summed in bfloat16 or wider, within the bound.
A program may use at most 128 MiB of HBM per device.

```python
import math
import jax
import jax.numpy as jnp
import numpy as np
from jax import lax

D = 1024
H = 8
DH = 128
BLK = 512
HB_DEV = 2
CAND_DEV = 64
USERS = 8
NBLK = 64
HIST = 32768
CANDS = 2048
NEED = 16
OWN = 16
CAP = 3
N_HIST = 32
N_USER = 8


def touch_ends(array, key, least, top_value):
    extent = array.shape
    index_at = [jax.random.randint(jax.random.fold_in(key, axis), (), 0, extent[axis]) for axis in range(len(extent))]
    array = array.at[tuple(index_at)].set(least)
    longest = extent.index(max(extent))
    index_at[longest] = (index_at[longest] + 1) % extent[longest]
    return array.at[tuple(index_at)].set(top_value)


def levels(key, shape, cuts, low, largest):
    def one(dim, blocks):
        draws = jax.random.uniform(jax.random.fold_in(jax.random.fold_in(key, 6), dim), (blocks,), jnp.float32, low / len(cuts), largest / len(cuts))
        return jnp.repeat(jnp.exp(draws), shape[dim] // blocks).reshape((-1,) + (1,) * (len(shape) - dim - 1))

    level = one(*cuts[0])
    for cut in cuts[1:]:
        level = level * one(*cut)
    return level


def profile(amount, total, limit, lean):
    loads = [(1 << 20) // math.isqrt(grade ** lean) + 1 for grade in range(2, amount + 1)]
    spare, given = total - limit - (amount - 1), [1] * (amount - 1)
    while spare > 0:
        candidates = [i for i in range(amount - 1) if given[i] < limit]
        pool, left = sum([loads[i] for i in candidates]), spare
        for i in candidates:
            addition = min(limit - given[i], max(1, left * loads[i] // pool), spare)
            given[i] = given[i] + addition
            spare = spare - addition
    return np.array([limit] + given)


def uneven(stream_key, number_of, total, bound, slope):
    if number_of == 2:
        one = jax.random.randint(stream_key, (), max(1, total - bound), min(bound, total - 1) + 1)
        return jnp.stack([one, total - one])
    tallies = jnp.asarray(profile(number_of, total, bound, slope), jnp.int32)
    couples = (number_of - 1) // 2
    donor, receiver = tallies[1:1 + 2 * couples:2], tallies[2:2 + 2 * couples:2]
    slack = jnp.minimum(donor - 1, bound - receiver)
    passed = jax.random.randint(jax.random.fold_in(stream_key, 1), (couples,), 0, 1 << 20) % (slack + 1)
    tallies = tallies.at[1:1 + 2 * couples:2].set(donor - passed).at[2:2 + 2 * couples:2].set(receiver + passed)
    return tallies[jax.random.permutation(jax.random.fold_in(stream_key, 2), number_of)]


def assign_block(own_key, own, number, rows, number_of, top, reach, slope):
    ranking = jax.random.permutation(own_key, number_of)
    packed, common = shares(number_of, rows * top, reach, slope, True), shares(number_of, rows * top, reach, slope, False)
    places = jnp.arange(number_of)

    def named(lengths, offset_by):
        used = int((lengths > 0).sum())
        fixed = max(1, used // 4)
        passed = fixed + (places - fixed + offset_by * (used - fixed)) % max(1, number_of - fixed)
        return jnp.zeros((number_of,), jnp.int32).at[ranking[jnp.where(places < fixed, places, passed)]].set(jnp.asarray(lengths, jnp.int32))

    lengths = jnp.where(number % 4 == 0, named(packed, number // 4), named(common, number - number // 4 - 1))
    mixed = jax.random.permutation(jax.random.fold_in(own, 3), number_of)
    source_of, sink = mixed[0:number_of // 2 * 2:2], mixed[1:number_of // 2 * 2:2]
    room = jnp.minimum(lengths[source_of] - 1, reach - lengths[sink]) // 2
    room = jnp.where((source_of == ranking[0]) | (sink == ranking[0]) | (lengths[sink] == 0), 0, jnp.maximum(room, 0))
    passed = jax.random.randint(jax.random.fold_in(own, 4), (number_of // 2,), 0, 1 << 20) % (room + 1)
    lengths = lengths.at[source_of].add(-passed).at[sink].add(passed)
    labels = jnp.searchsorted(jnp.cumsum(lengths), jnp.arange(rows * top), side="right").astype(jnp.int32)
    grid = labels.reshape(top, rows).T
    grid = grid[jax.random.permutation(jax.random.fold_in(own, 1), rows)]
    offset_by = jax.random.randint(jax.random.fold_in(own, 2), (rows, 1), 0, top)
    return jnp.take_along_axis(grid, (jnp.arange(top)[None, :] + offset_by) % top, axis=1)


def shares(number_of, total, reach, skew, full):
    portions = [(1 << 20) // math.isqrt(rank ** skew) + 1 for rank in range(1, number_of + 1)]
    largest = reach if full else min(reach, max(-(-total // number_of), total * portions[0] // sum(portions)))
    least = 1 if total - largest >= number_of - 1 else 0
    given, rest = [largest] + [least] * (number_of - 1), total - largest - least * (number_of - 1)
    while rest > 0:
        movable = [i for i in range(1, number_of) if given[i] < largest] or [i for i in range(1, number_of) if given[i] < reach]
        mass, remaining = sum([portions[i] for i in movable]), rest
        for i in movable:
            more = min(reach - given[i], max(1, remaining * portions[i] // mass), rest)
            given[i] = given[i] + more
            rest = rest - more
    return np.array(given)


def bell_draw(rng, shape, scale, reach, shards=(), held_as=jnp.bfloat16):
    values = scale * jax.random.normal(rng, shape, jnp.float32)
    if shards:
        values = values * levels(rng, shape, shards, -0.22, 0.18)
    return jnp.clip(values, -reach, reach).astype(held_as)


def setup_inputs(seed: int = 0) -> dict:
    splits = jax.random.split(jax.random.key(seed), 10)
    candidate_proj = bell_draw(splits[0], (USERS, CANDS, 4 * D), 1.0, 6.0, ((0, 8), (1, 32)))
    history_cache = bell_draw(splits[1], (N_HIST, USERS * OWN, BLK, 2 * DH), 1.0, 6.0, ((0, 32), (1, 8)))
    request_owner_keys = jax.random.split(jax.random.fold_in(splits[2], 1), USERS * (NBLK * H) // NEED)
    request_owner_turns = jax.random.permutation(jax.random.fold_in(splits[2], 3), USERS * (NBLK * H) // NEED)
    request_owner = jax.vmap(lambda own, number: assign_block(jax.random.fold_in(splits[2], 2), own, number, NEED, N_USER, 1, CAP, 2))(request_owner_keys, request_owner_turns).reshape((USERS, NBLK * H, 1))
    request_page = touch_ends(jax.random.randint(splits[3], (USERS, NBLK * H), 0, OWN), jax.random.fold_in(splits[3], 1), 0, OWN - 1).astype(jnp.int32)
    history_length = uneven(splits[4], USERS, (USERS * HIST) // 2 + USERS, HIST, 2).astype(jnp.int32)
    candidate_count = uneven(splits[5], USERS, (3 * USERS * CANDS) // 4 + USERS, CANDS, 2).astype(jnp.int32)
    block_mask = touch_ends((jax.random.randint(splits[6], (USERS, N_HIST, NBLK), 0, 4) < 3).astype(jnp.int32), jax.random.fold_in(splits[6], 1), 0, 1)
    norm_gain = jnp.clip(1.0 + 0.15 * jax.random.normal(splits[7], (D,), jnp.float32), 0.25, 1.75)
    w_out = bell_draw(splits[8], (D, D), D ** -0.5, 0.1875)
    return dict(candidate_proj=candidate_proj, history_cache=history_cache, request_owner=request_owner, request_page=request_page, history_length=history_length, candidate_count=candidate_count, block_mask=block_mask, norm_gain=norm_gain, w_out=w_out)


def reference(candidate_proj, history_cache, request_owner, request_page, history_length, candidate_count, block_mask, norm_gain, w_out):
    score_scale = DH ** (-0.5)
    group_blocks = math.gcd(NBLK, 8)
    group_events = group_blocks * BLK

    def one_user(user_index):
        activated = jax.nn.silu(candidate_proj[user_index].astype(jnp.float32))
        gating = activated[:, :D]
        cand_values = activated[:, D:2 * D].astype(jnp.bfloat16)
        queries = activated[:, 2 * D:3 * D].astype(jnp.bfloat16)
        cand_keys = activated[:, 3 * D:].astype(jnp.bfloat16)
        owners = request_owner[user_index, :, 0]
        page_list = request_page[user_index]
        columns = jnp.arange(NBLK * H, dtype=jnp.int32) // NEED
        pages_read = history_cache[columns, owners * OWN + page_list]
        history = pages_read.reshape(N_HIST, HB_DEV, H, BLK, 2 * DH).transpose(2, 0, 1, 3, 4).reshape(H, HIST, 2 * DH)
        tile_rows = jnp.arange(CANDS, dtype=jnp.int32) // CAND_DEV
        row_mask = block_mask[user_index][tile_rows].astype(jnp.float32)
        in_history = (jnp.arange(HIST, dtype=jnp.int32) < history_length[user_index]).astype(jnp.float32)

        def one_head(head_index):
            head_rows = history[head_index]
            head_queries = lax.dynamic_slice_in_dim(queries, head_index * DH, DH, 1)

            def step(totals, step_index):
                first = step_index * group_events
                page_rows = lax.dynamic_slice_in_dim(head_rows, first, group_events, 0)
                scores = lax.dot_general(head_queries, page_rows[:, :DH], (((1,), (1,)), ((), ())), preferred_element_type=jnp.float32) * score_scale
                block_part = lax.dynamic_slice_in_dim(row_mask, step_index * group_blocks, group_blocks, 1)
                weights_full = jnp.repeat(block_part, BLK, axis=1) * lax.dynamic_slice_in_dim(in_history, first, group_events, 0)[None, :]
                weighted = (jax.nn.silu(scores) * weights_full).astype(jnp.bfloat16)
                return (totals + jnp.dot(weighted, page_rows[:, DH:], preferred_element_type=jnp.float32), None)
            totals, unused = lax.scan(step, jnp.zeros((CANDS, DH), jnp.float32), jnp.arange(NBLK // group_blocks, dtype=jnp.int32))
            return totals
        attended = lax.map(one_head, jnp.arange(H, dtype=jnp.int32)).transpose(1, 0, 2).reshape(CANDS, D)
        self_scores = lax.optimization_barrier(jnp.sum((queries.astype(jnp.float32) * cand_keys.astype(jnp.float32)).reshape(CANDS, H, DH), axis=2)) * score_scale
        own_term = (jax.nn.silu(self_scores)[:, :, None] * cand_values.astype(jnp.float32).reshape(CANDS, H, DH)).reshape(CANDS, D)
        attn_sum = attended + own_term
        centre = attn_sum - lax.optimization_barrier(jnp.mean(attn_sum, axis=1, keepdims=True))
        variance = lax.optimization_barrier(jnp.mean(centre * centre, axis=1, keepdims=True))
        mixed = (centre * lax.rsqrt(variance + 1e-05) * norm_gain * gating).astype(jnp.bfloat16)
        result = jnp.dot(mixed, w_out, preferred_element_type=jnp.float32)
        live_rows = jnp.arange(CANDS, dtype=jnp.int32) < candidate_count[user_index]
        return jnp.where(live_rows[:, None], result, jnp.zeros_like(result)).astype(jnp.bfloat16)
    return lax.map(one_user, jnp.arange(USERS, dtype=jnp.int32))
```

```python
import jax
import jax.numpy as jnp
from jax import lax
from jax.experimental import pallas as pl
from jax.experimental.pallas import tpu as pltpu
from jax.sharding import PartitionSpec as P

D = 1024
H = 8
DH = 128
BLK = 512
TILE = 64
NY = 4
NZ = 8
PEERS = 8
CAP = 3
PAGES = 16
SLOTS = PEERS * CAP
LAG = 2
SCALE = DH ** (-0.5)
MESH = pl.DeviceIdType.MESH


def silu(v):
    half = v * 0.5
    return half * jnp.tanh(half) + half


def kernel(
    length_ref,
    count_ref,
    bmask,
    proj,
    owner_col,
    owner_row,
    page_col,
    gain,
    cache,
    w_out,
    result,
    cache_v,
    w_v,
    stage,
    pages,
    queries,
    partial,
    gating,
    own_term,
    msg,
    asked,
    msg_s,
    asked_s,
    rs_send,
    rs_recv,
    xs_send,
    xs_recv,
    local_sem,
    req_send,
    req_recv,
    page_send,
    page_recv,
    pair_send,
    pair_recv,
    info_sem,
    ag_send,
    ag_recv,
    sum_send,
    sum_recv,
    x_sem,
):
    hist, user = lax.axis_index("hist"), lax.axis_index("user")
    xh, z, core = hist // 16, (hist // 2) % NZ, hist % 2
    xl, y = user // NY, user % NY

    def at(xh_, z_, core_):
        return (xh_ * 16 + z_ * 2 + core_, user)

    up, down = at(xh, (z + 1) % NZ, core), at(xh, (z + 7) % NZ, core)
    across, pair = at(1 - xh, z, core), at(xh, z, 1 - core)

    def owner_at(d):
        return (hist, ((xl + d // NY) % 2) * NY + (y + d % NY) % NY)

    def asker_at(d):
        return (hist, ((xl + d // NY) % 2) * NY + (y + NY - d % NY) % NY)

    def remote(src, dst, send, recv, device):
        return pltpu.make_async_remote_copy(
            src_ref=src, dst_ref=dst, send_sem=send, recv_sem=recv, device_id=device, device_id_type=MESH
        )

    load_cache = pltpu.make_async_copy(cache, cache_v, local_sem.at[0])
    load_cache.start()
    load_w = pltpu.make_async_copy(w_out, w_v, local_sem.at[1])
    load_w.start()

    barrier = pltpu.get_barrier_semaphore()
    for d in range(1, PEERS):
        pl.semaphore_signal(barrier, inc=1, device_id=asker_at(d), device_id_type=MESH)
    for device in (up, down, across, pair):
        pl.semaphore_signal(barrier, inc=1, device_id=device, device_id_type=MESH)

    row = lax.broadcasted_iota(jnp.int32, (16, 128), 0)
    lane = lax.broadcasted_iota(jnp.int32, (16, 128), 1)
    owners = jnp.broadcast_to(owner_col[...], (16, 128))
    same = (owners == jnp.broadcast_to(owner_row[...], (16, 128))) & (lane < row)
    rank = jnp.minimum(jnp.sum(same.astype(jnp.int32), axis=1, keepdims=True), CAP - 1)
    place = (((owners >> 2) ^ xl) & 1) * NY + ((owners - y) & 3)
    slot = jnp.broadcast_to(rank, (16, 128)) * PEERS + place
    match = slot == lane
    want = jnp.broadcast_to(page_col[...], (16, 128))
    valid = jnp.clip(length_ref[0] - (hist * 2 + (row >> 3)) * BLK, 0, BLK)
    zero = jnp.zeros((16, 128), jnp.int32)

    def pick(values):
        return jnp.sum(jnp.where(match, values, zero), axis=0, keepdims=True)

    r8 = lax.broadcasted_iota(jnp.int32, (8, 128), 0)
    wanted = jnp.clip(pick(want), 0, PAGES - 1)
    heads = jnp.clip(pick(row & 7), 0, H - 1)
    first = jnp.where(r8 == 0, wanted, jnp.where(r8 == 1, heads, pick(valid)))
    msg[0, 0:8, :] = first
    msg[0, 8:24, :] = slot

    for e in range(H):
        q = silu(proj[:, 2 * D + e * DH : 2 * D + (e + 1) * DH].astype(jnp.float32))
        queries[z, xh, e] = q.astype(jnp.bfloat16)

    pl.semaphore_wait(barrier, PEERS - 1 + 4)

    ask = []
    for d in range(1, PEERS):
        ask.append(remote(msg.at[0, 0:8], asked.at[d], req_send.at[d], req_recv.at[d], owner_at(d)))
    for copy in ask:
        copy.start()
    ag_x = remote(queries.at[z, xh], queries.at[z, xh], ag_send.at[0, 4], ag_recv.at[0, 4], across)
    ag_x.start()
    tell = remote(msg.at[0], msg.at[1], info_sem.at[0], info_sem.at[1], pair)
    tell.start()
    load_cache.wait()
    for copy in ask:
        copy.wait_recv()
    copy_asked = pltpu.make_async_copy(asked.at[pl.ds(1, PEERS - 1)], asked_s.at[pl.ds(1, PEERS - 1)], local_sem.at[2])
    copy_asked.start()
    tell.wait()
    copy_msg = pltpu.make_async_copy(msg, msg_s, local_sem.at[3])
    copy_msg.start()
    copy_asked.wait()
    copy_msg.wait()

    def page_copy(k, d):
        i = k * PEERS + d
        return remote(stage.at[i], pages.at[0, i], page_send.at[i], page_recv.at[i], asker_at(d))

    def serve(k, carry):
        for d in (4, 1, 3, 5, 7, 2, 6):
            stage[k * PEERS + d] = cache_v[asked_s[d, 0, k * PEERS + d]]
            page_copy(k, d).start()
        pages[0, k * PEERS] = cache_v[msg_s[0, 0, k * PEERS]]
        return carry

    lax.fori_loop(0, CAP, serve, 0)

    ag_x.wait()

    def gather_step(s):
        zu, zd = (z + NZ - s) % NZ, (z + s) % NZ
        if s < 3:
            up_part, down_part = queries.at[zu], queries.at[zd]
        else:
            up_part, down_part = queries.at[zu, 0], queries.at[zd, 1]
        return (
            remote(up_part, up_part, ag_send.at[0, s], ag_recv.at[0, s], up),
            remote(down_part, down_part, ag_send.at[1, s], ag_recv.at[1, s], down),
        )

    steps = [gather_step(s) for s in range(4)]
    for copy in steps[0]:
        copy.start()

    gating[...] = silu(proj[:, 0:D].astype(jnp.float32))
    for e in range(H):
        cols = slice(e * DH, (e + 1) * DH)
        v = silu(proj[:, D + e * DH : D + (e + 1) * DH].astype(jnp.float32)).astype(jnp.bfloat16)
        k = silu(proj[:, 3 * D + e * DH : 3 * D + (e + 1) * DH].astype(jnp.float32)).astype(jnp.bfloat16)
        q = queries[z, xh, e]
        score = jnp.sum(q.astype(jnp.float32) * k.astype(jnp.float32), axis=1, keepdims=True) * SCALE
        own_term[:, cols] = silu(score) * v.astype(jnp.float32)

    for s in range(4):
        for direction in range(2):
            steps[s][direction].wait_recv()
            if s < 3:
                steps[s + 1][direction].start()

    def pair_copy(i):
        return remote(pages.at[0, i], pages.at[1, i], pair_send.at[i], pair_recv.at[i], pair)

    rows = lax.broadcasted_iota(jnp.int32, (BLK, DH), 0)
    chunk = 512

    def attend(t, carry):
        side = t % 2
        i = t // 2 - side * LAG

        @pl.when((i >= 0) & (i < SLOTS))
        def _():
            @pl.when((side == 0) & (i % PEERS != 0))
            def _():
                page_copy(0, i).wait_recv()

            @pl.when(side == 0)
            def _():
                pair_copy(i).start()

            @pl.when(side == 1)
            def _():
                pair_copy(i).wait_recv()

            head = msg_s[side, 1, i]
            live = msg_s[side, 2, i]
            k = pages[side, i, :, 0:DH]
            v = pages[side, i, :, DH : 2 * DH]
            v = jnp.where(rows < live, v, jnp.zeros_like(v))
            n = chunk // 128
            for j in range(1024 // chunk):
                q = queries[j * n : (j + 1) * n, :, head].reshape(chunk, DH)
                score = lax.dot_general(q, k, (((1,), (1,)), ((), ())), preferred_element_type=jnp.float32)
                half = score * (SCALE * 0.5)
                weight = (half * jnp.tanh(half) + half).astype(jnp.bfloat16)
                term = jnp.dot(weight, v, preferred_element_type=jnp.float32)
                partial[side, i, j * chunk : (j + 1) * chunk, :] = term.astype(jnp.bfloat16)

        return carry

    lax.fori_loop(0, 2 * (SLOTS + LAG), attend, 0)

    def term_of(zd, xd, e):
        total = None
        tile = xd * 16 + zd * 2 + core
        for side in range(2):
            other = core if side == 0 else 1 - core
            for b in range(2):
                block = (hist - core + other) * 2 + b
                m = bmask[tile, block].astype(jnp.float32)
                s = msg_s[side, 8 + b * H + e, 0]
                part = partial[side, s, pl.ds(pl.multiple_of(zd * 128 + xd * 64, 64), TILE), :]
                part = part.astype(jnp.float32) * m
                total = part if total is None else total + part
        return total

    def sum_copy(g, s, j):
        return remote(
            rs_send.at[g, s, j], rs_recv.at[g, s, j], sum_send.at[g, s, j], sum_recv.at[g, s, j], up if g == 0 else down
        )

    def ring_step(s, arrived):
        for j in range(2):
            for g in range(2):
                zd = (z + NZ - 1 - s) % NZ if g == 0 else (z + 1 + s) % NZ
                terms = [term_of(zd, j, g * 4 + e) for e in range(4)]
                if arrived:
                    sum_copy(g, s - 1, j).wait_recv()
                for e in range(4):
                    cols = slice(e * DH, (e + 1) * DH)
                    v = terms[e]
                    if arrived:
                        v = v + rs_recv[g, s - 1, j, :, cols].astype(jnp.float32)
                    rs_send[g, s, j, :, cols] = v.astype(jnp.bfloat16)
                sum_copy(g, s, j).start()

    ring_step(0, False)

    def ring_body(s, carry):
        ring_step(s, True)
        return carry

    lax.fori_loop(1, NZ - 1, ring_body, 0)
    load_w.wait()
    for j in range(2):
        for g in range(2):
            sum_copy(g, NZ - 2, j).wait_recv()

    def final_terms(xd):
        out = []
        for e in range(H):
            g, cols = e // 4, slice(e % 4 * DH, (e % 4 + 1) * DH)
            out.append(term_of(z, xd, e) + rs_recv[g, NZ - 2, xd, :, cols].astype(jnp.float32))
        return out

    for e, v in enumerate(final_terms(1 - xh)):
        xs_send[:, e * DH : (e + 1) * DH] = v.astype(jnp.bfloat16)
    x_copy = remote(xs_send, xs_recv, x_sem.at[0], x_sem.at[1], across)
    x_copy.start()
    for e, v in enumerate(final_terms(xh)):
        cols = slice(e * DH, (e + 1) * DH)
        own_term[:, cols] = own_term[:, cols] + v
    x_copy.wait()
    attn = own_term[...] + xs_recv[...].astype(jnp.float32)
    centre = attn - jnp.mean(attn, axis=1, keepdims=True)
    variance = jnp.mean(centre * centre, axis=1, keepdims=True)
    mixed = (centre * lax.rsqrt(variance + 1e-05) * gain[...] * gating[...]).astype(jnp.bfloat16)
    out = jnp.dot(mixed, w_v[...], preferred_element_type=jnp.float32)
    live_row = hist * TILE + lax.broadcasted_iota(jnp.int32, (TILE, D), 0) < count_ref[0]
    result[...] = jnp.where(live_row, out, jnp.zeros_like(out)).astype(jnp.bfloat16)

    for copy in ask:
        copy.wait_send()
    for s in range(4):
        for direction in range(2):
            steps[s][direction].wait_send()

    def drain_pages(k, carry):
        for d in range(PEERS):
            if d:
                page_copy(k, d).wait_send()
            pair_copy(k * PEERS + d).wait_send()
        return carry

    lax.fori_loop(0, CAP, drain_pages, 0)

    def drain_sums(s, carry):
        for g in range(2):
            for j in range(2):
                sum_copy(g, s, j).wait_send()
        return carry

    lax.fori_loop(0, NZ - 1, drain_sums, 0)


def body(proj, cache, owner, page, length, count, bmask, gain, w_out):
    vmem, smem = pl.BlockSpec(memory_space=pltpu.VMEM), pl.BlockSpec(memory_space=pltpu.SMEM)
    anywhere = pl.BlockSpec(memory_space=pl.ANY)
    owner_col = owner[0]
    owner_row = jnp.pad(owner.reshape(1, 16), ((0, 0), (0, 112)), constant_values=-1)
    page_col = page.reshape(16, 1)
    dma = pltpu.SemaphoreType.DMA
    bf, f32, i32 = jnp.bfloat16, jnp.float32, jnp.int32
    out = pl.pallas_call(
        kernel,
        out_shape=jax.ShapeDtypeStruct((TILE, D), bf),
        in_specs=[smem, smem, smem, vmem, vmem, vmem, vmem, vmem, anywhere, anywhere],
        out_specs=vmem,
        scratch_shapes=[
            pltpu.VMEM((16, BLK, 2 * DH), bf),
            pltpu.VMEM((D, D), bf),
            pltpu.VMEM((SLOTS, BLK, 2 * DH), bf),
            pltpu.VMEM((2, SLOTS, BLK, 2 * DH), bf),
            pltpu.VMEM((NZ, 2, H, TILE, DH), bf),
            pltpu.VMEM((2, SLOTS, 1024, DH), bf),
            pltpu.VMEM((TILE, D), f32),
            pltpu.VMEM((TILE, D), f32),
            pltpu.VMEM((2, 24, 128), i32),
            pltpu.VMEM((PEERS, 8, 128), i32),
            pltpu.SMEM((2, 24, 128), i32),
            pltpu.SMEM((PEERS, 8, 128), i32),
            pltpu.VMEM((2, NZ - 1, 2, TILE, D // 2), bf),
            pltpu.VMEM((2, NZ - 1, 2, TILE, D // 2), bf),
            pltpu.VMEM((TILE, D), bf),
            pltpu.VMEM((TILE, D), bf),
            dma((4,)),
            dma((PEERS,)),
            dma((PEERS,)),
            dma((SLOTS,)),
            dma((SLOTS,)),
            dma((SLOTS,)),
            dma((SLOTS,)),
            dma((2,)),
            dma((2, 5)),
            dma((2, 5)),
            dma((2, NZ - 1, 2)),
            dma((2, NZ - 1, 2)),
            dma((2,)),
        ],
        compiler_params=pltpu.CompilerParams(
            collective_id=0, has_side_effects=True, vmem_limit_bytes=60 * 1024 * 1024
        ),
        name="score_candidates",
    )(length, count, bmask[0], proj[0], owner_col, owner_row, page_col, gain.reshape(1, D), cache[0], w_out)
    return out[None]


def solution(mesh):
    return jax.shard_map(
        body,
        mesh=mesh,
        in_specs=(
            P("user", "hist", None),
            P("hist", "user", None, None),
            P("user", "hist", None),
            P("user", "hist"),
            P("user"),
            P("user"),
            P("user", None, None),
            P(),
            P(),
        ),
        out_specs=P("user", "hist", None),
        check_vma=False,
    )
```

```python
import jax
import jax.numpy as jnp
from jax import lax
from jax.experimental import pallas as pl
from jax.experimental.pallas import tpu as pltpu
from jax.sharding import PartitionSpec as P

D = 1024
H = 8
DH = 128
BLK = 512
TILE = 64
NY = 4
NZ = 8
PEERS = 8
CAP = 3
PAGES = 16
SLOTS = PEERS * CAP
LAG = 2
SCALE = DH ** (-0.5)
MESH = pl.DeviceIdType.MESH


def silu(v):
    half = v * 0.5
    return half * jnp.tanh(half) + half


def kernel(
    length_hbm,
    count_hbm,
    owner_ref,
    page_ref,
    gain,
    bmask_hbm,
    proj_hbm,
    cache,
    w_out,
    result,
    length_ref,
    count_ref,
    bmask,
    seen,
    proj,
    cache_v,
    w_v,
    stage,
    pages,
    queries,
    partial,
    gating,
    own_term,
    msg,
    asked,
    msg_s,
    asked_s,
    za_send,
    za_recv,
    zb_send,
    zb_recv,
    xb_send,
    xb_recv,
    xa_send,
    xa_recv,
    local_sem,
    req_send,
    req_recv,
    page_send,
    page_recv,
    pair_send,
    pair_recv,
    info_sem,
    ag_send,
    ag_recv,
    za_ssem,
    za_rsem,
    zb_ssem,
    zb_rsem,
    xb_ssem,
    xb_rsem,
    xa_sem,
):
    hist, user = lax.axis_index("hist"), lax.axis_index("user")
    xh, z, core = hist // 16, (hist // 2) % NZ, hist % 2
    xl, y = user // NY, user % NY

    def at(xh_, z_, core_):
        return (xh_ * 16 + z_ * 2 + core_, user)

    up, down = at(xh, (z + 1) % NZ, core), at(xh, (z + 7) % NZ, core)
    across, pair = at(1 - xh, z, core), at(xh, z, 1 - core)

    def owner_at(d):
        return (hist, ((xl + d // NY) % 2) * NY + (y + d % NY) % NY)

    def asker_at(d):
        return (hist, ((xl + d // NY) % 2) * NY + (y + NY - d % NY) % NY)

    def remote(src, dst, send, recv, device):
        return pltpu.make_async_remote_copy(
            src_ref=src, dst_ref=dst, send_sem=send, recv_sem=recv, device_id=device, device_id_type=MESH
        )

    load_length = pltpu.make_async_copy(length_hbm, length_ref, local_sem.at[6])
    load_length.start()
    load_count = pltpu.make_async_copy(count_hbm, count_ref, local_sem.at[7])
    load_count.start()
    load_cache = pltpu.make_async_copy(cache, cache_v, local_sem.at[0])
    load_cache.start()
    load_proj = pltpu.make_async_copy(proj_hbm, proj, local_sem.at[4])
    load_proj.start()
    load_mask = pltpu.make_async_copy(bmask_hbm, bmask, local_sem.at[5])
    load_mask.start()
    load_w = pltpu.make_async_copy(w_out, w_v, local_sem.at[1])
    load_w.start()

    barrier = pltpu.get_barrier_semaphore()
    for d in range(1, PEERS):
        pl.semaphore_signal(barrier, inc=1, device_id=asker_at(d), device_id_type=MESH)
    for device in (up, down, across, pair):
        pl.semaphore_signal(barrier, inc=1, device_id=device, device_id_type=MESH)

    row = lax.broadcasted_iota(jnp.int32, (16, 128), 0)
    lane = lax.broadcasted_iota(jnp.int32, (16, 128), 1)
    zero = jnp.zeros((16, 128), jnp.int32)
    owners, owners_across, want = zero, zero - 1, zero
    for r in range(16):
        owners = jnp.where(row == r, owner_ref[0, r], owners)
        owners_across = jnp.where(lane == r, owner_ref[0, r], owners_across)
        want = jnp.where(row == r, page_ref[0, r], want)
    same = (owners == owners_across) & (lane < row)
    rank = jnp.minimum(jnp.sum(same.astype(jnp.int32), axis=1, keepdims=True), CAP - 1)
    place = (((owners >> 2) ^ xl) & 1) * NY + ((owners - y) & 3)
    slot = jnp.broadcast_to(rank, (16, 128)) * PEERS + place
    match = slot == lane
    load_length.wait()
    valid = jnp.clip(length_ref[0] - (hist * 2 + (row >> 3)) * BLK, 0, BLK)

    def pick(values):
        return jnp.sum(jnp.where(match, values, zero), axis=0, keepdims=True)

    r8 = lax.broadcasted_iota(jnp.int32, (8, 128), 0)
    wanted = jnp.clip(pick(want), 0, PAGES - 1)
    heads = jnp.clip(pick(row & 7), 0, H - 1)
    blocks = jnp.clip(pick(row >> 3), 0, 1)
    first = jnp.where(r8 == 0, wanted, jnp.where(r8 == 1, heads, jnp.where(r8 == 2, pick(valid), blocks)))
    msg[0, 0:8, :] = first
    msg[0, 8:24, :] = slot

    pl.semaphore_wait(barrier, PEERS - 1 + 4)

    ask = []
    for d in range(1, PEERS):
        ask.append(remote(msg.at[0, 0:8], asked.at[d], req_send.at[d], req_recv.at[d], owner_at(d)))
    for copy in ask:
        copy.start()
    tell = remote(msg.at[0], msg.at[1], info_sem.at[0], info_sem.at[1], pair)
    tell.start()
    load_proj.wait()
    for e in range(H):
        q = silu(proj[:, 2 * D + e * DH : 2 * D + (e + 1) * DH].astype(jnp.float32))
        queries[z, xh, e] = q.astype(jnp.bfloat16)

    ag_x = remote(queries.at[z, xh], queries.at[z, xh], ag_send.at[0, 4], ag_recv.at[0, 4], across)
    ag_x.start()
    for copy in ask:
        copy.wait_recv()
    copy_asked = pltpu.make_async_copy(asked.at[pl.ds(1, PEERS - 1)], asked_s.at[pl.ds(1, PEERS - 1)], local_sem.at[2])
    copy_asked.start()
    load_cache.wait()
    copy_asked.wait()

    def page_copy(k, d):
        i = k * PEERS + d
        return remote(stage.at[i], pages.at[0, i], page_send.at[i], page_recv.at[i], asker_at(d))

    def serve(k, carry):
        for d in (4, 1, 3, 5, 7, 2, 6):
            stage[k * PEERS + d] = cache_v[asked_s[d, 0, k * PEERS + d]]
            page_copy(k, d).start()
        return carry

    lax.fori_loop(0, CAP, serve, 0)
    tell.wait()
    copy_msg = pltpu.make_async_copy(msg, msg_s, local_sem.at[3])
    copy_msg.start()

    ag_x.wait()

    def gather_step(s):
        zu, zd = (z + NZ - s) % NZ, (z + s) % NZ
        if s < 3:
            up_part, down_part = queries.at[zu], queries.at[zd]
        else:
            up_part, down_part = queries.at[zu, 0], queries.at[zd, 1]
        return (
            remote(up_part, up_part, ag_send.at[0, s], ag_recv.at[0, s], up),
            remote(down_part, down_part, ag_send.at[1, s], ag_recv.at[1, s], down),
        )

    steps = [gather_step(s) for s in range(4)]
    for copy in steps[0]:
        copy.start()

    gating[...] = silu(proj[:, 0:D].astype(jnp.float32))
    for e in range(H):
        cols = slice(e * DH, (e + 1) * DH)
        v = silu(proj[:, D + e * DH : D + (e + 1) * DH].astype(jnp.float32)).astype(jnp.bfloat16)
        k = silu(proj[:, 3 * D + e * DH : 3 * D + (e + 1) * DH].astype(jnp.float32)).astype(jnp.bfloat16)
        q = queries[z, xh, e]
        score = jnp.sum(q.astype(jnp.float32) * k.astype(jnp.float32), axis=1, keepdims=True) * SCALE
        own_term[:, cols] = silu(score) * v.astype(jnp.float32)

    load_mask.wait()

    def see(n, carry):
        zd, xd = n // 2, n % 2
        for side in range(2):
            for b in range(2):
                other = core if side == 0 else 1 - core
                m = bmask[xd * 16 + zd * 2 + core, (hist - core + other) * 2 + b].astype(jnp.float32)
                seen[side, b, pl.ds(pl.multiple_of(n * TILE, TILE), TILE), :] = jnp.full((TILE, DH), m, jnp.float32)
        return carry

    lax.fori_loop(0, 2 * NZ, see, 0)
    copy_msg.wait()
    for k in range(CAP):
        pages[0, k * PEERS] = cache_v[msg_s[0, 0, k * PEERS]]

    for s in range(4):
        for direction in range(2):
            steps[s][direction].wait_recv()
            if s < 3:
                steps[s + 1][direction].start()

    def pair_copy(i):
        return remote(pages.at[0, i], pages.at[1, i], pair_send.at[i], pair_recv.at[i], pair)

    rows = lax.broadcasted_iota(jnp.int32, (BLK, DH), 0)
    chunk = 512

    def attend(t, carry):
        side = t % 2
        i = t // 2 - side * LAG

        @pl.when((i >= 0) & (i < SLOTS))
        def _():
            @pl.when((side == 0) & (i % PEERS != 0))
            def _():
                page_copy(0, i).wait_recv()

            @pl.when(side == 0)
            def _():
                pair_copy(i).start()

            @pl.when(side == 1)
            def _():
                pair_copy(i).wait_recv()

            head = msg_s[side, 1, i]
            live = msg_s[side, 2, i]
            block = msg_s[side, 3, i]
            k = pages[side, i, :, 0:DH]
            v = pages[side, i, :, DH : 2 * DH]
            v = jnp.where(rows < live, v, jnp.zeros_like(v))
            n = chunk // 128
            for j in range(1024 // chunk):
                q = queries[j * n : (j + 1) * n, :, head].reshape(chunk, DH)
                score = lax.dot_general(q, k, (((1,), (1,)), ((), ())), preferred_element_type=jnp.float32)
                half = score * (SCALE * 0.5)
                weight = (half * jnp.tanh(half) + half).astype(jnp.bfloat16)
                term = jnp.dot(weight, v, preferred_element_type=jnp.float32)
                span = slice(j * chunk, (j + 1) * chunk)
                partial[side, i, span, :] = (term * seen[side, block, span, :]).astype(jnp.bfloat16)

        return carry

    lax.fori_loop(0, 2 * (SLOTS + LAG), attend, 0)

    def term_of(zd, xd, e):
        total = None
        for side in range(2):
            for b in range(2):
                part = partial[side, msg_s[side, 8 + b * H + e, 0], pl.ds(pl.multiple_of(zd * 128 + xd * 64, 64), TILE), :]
                part = part.astype(jnp.float32)
                total = part if total is None else total + part
        return total

    def offset_of(g, s):
        return 4 - s if g == 0 else 4 + s

    def heads_of(g, s):
        return range(4) if s else range(2 * g, 2 * g + 2)

    def za_copy(g, s, j):
        part = pl.ds(heads_of(g, s)[0], len(heads_of(g, s)))
        return remote(
            za_send.at[g, s, j, part], za_recv.at[g, s, j, part], za_ssem.at[g, s, j], za_rsem.at[g, s, j], (up, down)[g]
        )

    def zb_copy(g, s):
        part = pl.ds(heads_of(g, s)[0], len(heads_of(g, s)))
        return remote(zb_send.at[g, s, part], zb_recv.at[g, s, part], zb_ssem.at[g, s], zb_rsem.at[g, s], (up, down)[g])

    def xb_copy(o):
        return remote(xb_send.at[o], xb_recv.at[o], xb_ssem.at[o], xb_rsem.at[o], across)

    def a_step(s):
        for j in range(2):
            for g in range(2):
                zd = (z + offset_of(g, s)) % NZ
                if s:
                    za_copy(g, s - 1, j).wait_recv()
                for e in heads_of(g, s):
                    v = term_of(zd, j, e)
                    if s and e in heads_of(g, s - 1):
                        v = v + za_recv[g, s - 1, j, e].astype(jnp.float32)
                    za_send[g, s, j, e] = v.astype(jnp.bfloat16)
                za_copy(g, s, j).start()

    def x_step(o):
        for e in range(4):
            xb_send[o, e] = term_of((z + o) % NZ, 1 - xh, 4 + e).astype(jnp.bfloat16)
        xb_copy(o).start()

    def b_step(s):
        for g in range(2):
            o = offset_of(g, s)
            if s or g == 0:
                xb_copy(o).wait_recv()
            if s:
                zb_copy(g, s - 1).wait_recv()
            for e in heads_of(g, s):
                v = term_of((z + o) % NZ, xh, 4 + e) + xb_recv[o, e].astype(jnp.float32)
                if s and e in heads_of(g, s - 1):
                    v = v + zb_recv[g, s - 1, e].astype(jnp.float32)
                zb_send[g, s, e] = v.astype(jnp.bfloat16)
            zb_copy(g, s).start()

    x_step(4)
    a_step(0)
    x_step(3)
    x_step(5)
    x_step(2)
    x_step(6)
    a_step(1)
    b_step(0)
    x_step(1)
    x_step(7)
    x_step(0)
    a_step(2)
    b_step(1)
    a_step(3)
    b_step(2)

    def a_final(xd, e):
        v = term_of(z, xd, e) + za_recv[0, 3, xd, e].astype(jnp.float32)
        return v + za_recv[1, 3, xd, e].astype(jnp.float32)

    for j in range(2):
        for g in range(2):
            za_copy(g, 3, j).wait_recv()
    for e in range(4):
        xa_send[e] = a_final(1 - xh, e).astype(jnp.bfloat16)
    xa_copy = remote(xa_send, xa_recv, xa_sem.at[0], xa_sem.at[1], across)
    xa_copy.start()
    b_step(3)
    for e in range(4):
        cols = slice(e * DH, (e + 1) * DH)
        own_term[:, cols] = own_term[:, cols] + a_final(xh, e)
    load_w.wait()
    load_count.wait()
    xa_copy.wait()
    for e in range(4):
        cols = slice(e * DH, (e + 1) * DH)
        own_term[:, cols] = own_term[:, cols] + xa_recv[e].astype(jnp.float32)
    xb_copy(0).wait_recv()
    for g in range(2):
        zb_copy(g, 3).wait_recv()
    for e in range(4):
        cols = slice((4 + e) * DH, (5 + e) * DH)
        v = term_of(z, xh, 4 + e) + xb_recv[0, e].astype(jnp.float32)
        v = v + zb_recv[0, 3, e].astype(jnp.float32) + zb_recv[1, 3, e].astype(jnp.float32)
        own_term[:, cols] = own_term[:, cols] + v
    attn = own_term[...]
    centre = attn - jnp.mean(attn, axis=1, keepdims=True)
    variance = jnp.mean(centre * centre, axis=1, keepdims=True)
    mixed = (centre * lax.rsqrt(variance + 1e-05) * gain[...] * gating[...]).astype(jnp.bfloat16)
    out = jnp.dot(mixed, w_v[...], preferred_element_type=jnp.float32)
    live_row = hist * TILE + lax.broadcasted_iota(jnp.int32, (TILE, D), 0) < count_ref[0]
    result[...] = jnp.where(live_row, out, jnp.zeros_like(out)).astype(jnp.bfloat16)

    for copy in ask:
        copy.wait_send()
    for s in range(4):
        for direction in range(2):
            steps[s][direction].wait_send()

    def drain_pages(k, carry):
        for d in range(PEERS):
            if d:
                page_copy(k, d).wait_send()
            pair_copy(k * PEERS + d).wait_send()
        return carry

    lax.fori_loop(0, CAP, drain_pages, 0)

    for s in range(4):
        for g in range(2):
            for j in range(2):
                za_copy(g, s, j).wait_send()
            zb_copy(g, s).wait_send()
    for o in range(NZ):
        xb_copy(o).wait_send()


def body(proj, cache, owner, page, length, count, bmask, gain, w_out):
    vmem, smem = pl.BlockSpec(memory_space=pltpu.VMEM), pl.BlockSpec(memory_space=pltpu.SMEM)
    anywhere = pl.BlockSpec(memory_space=pl.ANY)
    dma = pltpu.SemaphoreType.DMA
    bf, f32, i32 = jnp.bfloat16, jnp.float32, jnp.int32
    out = pl.pallas_call(
        kernel,
        out_shape=jax.ShapeDtypeStruct((TILE, D), bf),
        in_specs=[anywhere, anywhere, smem, smem, vmem, anywhere, anywhere, anywhere, anywhere],
        out_specs=vmem,
        scratch_shapes=[
            pltpu.SMEM((1,), i32),
            pltpu.SMEM((1,), i32),
            pltpu.SMEM((32, 64), i32),
            pltpu.VMEM((2, 2, 1024, DH), f32),
            pltpu.VMEM((TILE, 4 * D), bf),
            pltpu.VMEM((16, BLK, 2 * DH), bf),
            pltpu.VMEM((D, D), bf),
            pltpu.VMEM((SLOTS, BLK, 2 * DH), bf),
            pltpu.VMEM((2, SLOTS, BLK, 2 * DH), bf),
            pltpu.VMEM((NZ, 2, H, TILE, DH), bf),
            pltpu.VMEM((2, SLOTS, 1024, DH), bf),
            pltpu.VMEM((TILE, D), f32),
            pltpu.VMEM((TILE, D), f32),
            pltpu.VMEM((2, 24, 128), i32),
            pltpu.VMEM((PEERS, 8, 128), i32),
            pltpu.SMEM((2, 24, 128), i32),
            pltpu.SMEM((PEERS, 8, 128), i32),
            pltpu.VMEM((2, 4, 2, 4, TILE, DH), bf),
            pltpu.VMEM((2, 4, 2, 4, TILE, DH), bf),
            pltpu.VMEM((2, 4, 4, TILE, DH), bf),
            pltpu.VMEM((2, 4, 4, TILE, DH), bf),
            pltpu.VMEM((NZ, 4, TILE, DH), bf),
            pltpu.VMEM((NZ, 4, TILE, DH), bf),
            pltpu.VMEM((4, TILE, DH), bf),
            pltpu.VMEM((4, TILE, DH), bf),
            dma((8,)),
            dma((PEERS,)),
            dma((PEERS,)),
            dma((SLOTS,)),
            dma((SLOTS,)),
            dma((SLOTS,)),
            dma((SLOTS,)),
            dma((2,)),
            dma((2, 5)),
            dma((2, 5)),
            dma((2, 4, 2)),
            dma((2, 4, 2)),
            dma((2, 4)),
            dma((2, 4)),
            dma((NZ,)),
            dma((NZ,)),
            dma((2,)),
        ],
        compiler_params=pltpu.CompilerParams(
            collective_id=0, has_side_effects=True, vmem_limit_bytes=60 * 1024 * 1024
        ),
        name="score_candidates",
    )(length, count, owner.reshape(1, 16), page, gain.reshape(1, D), bmask[0], proj[0], cache[0], w_out)
    return out[None]


def solution(mesh):
    return jax.shard_map(
        body,
        mesh=mesh,
        in_specs=(
            P("user", "hist", None),
            P("hist", "user", None, None),
            P("user", "hist", None),
            P("user", "hist"),
            P("user"),
            P("user"),
            P("user", None, None),
            P(),
            P(),
        ),
        out_specs=P("user", "hist", None),
        check_vma=False,
    )
```

```python
import jax
import jax.numpy as jnp
from jax import lax
from jax.experimental import pallas as pl
from jax.experimental.pallas import tpu as pltpu
from jax.sharding import PartitionSpec as P

D = 1024
H = 8
DH = 128
BLK = 512
TILE = 64
NY = 4
NZ = 8
PEERS = 8
CAP = 3
PAGES = 16
SLOTS = PEERS * CAP
LAG = 1
ORDER = (0, 4, 1, 3, 5, 7, 2, 6)
SCALE = DH ** (-0.5)
MESH = pl.DeviceIdType.MESH


def silu(v):
    half = v * 0.5
    return half * jnp.tanh(half) + half


def kernel(
    length_hbm,
    count_hbm,
    owner_ref,
    page_ref,
    gain,
    bmask_hbm,
    proj_hbm,
    cache,
    w_out,
    result,
    length_ref,
    count_ref,
    bmask,
    seen,
    proj,
    cache_v,
    w_v,
    stage,
    pages,
    queries,
    partial,
    gating,
    own_term,
    msg,
    asked,
    msg_s,
    asked_s,
    za_send,
    za_recv,
    zb_send,
    zb_recv,
    xb_send,
    xb_recv,
    xa_send,
    xa_recv,
    local_sem,
    req_send,
    req_recv,
    page_send,
    page_recv,
    pair_send,
    pair_recv,
    info_sem,
    ag_send,
    ag_recv,
    za_ssem,
    za_rsem,
    zb_ssem,
    zb_rsem,
    xb_ssem,
    xb_rsem,
    xa_sem,
):
    hist, user = lax.axis_index("hist"), lax.axis_index("user")
    xh, z, core = hist // 16, (hist // 2) % NZ, hist % 2
    xl, y = user // NY, user % NY

    def at(xh_, z_, core_):
        return (xh_ * 16 + z_ * 2 + core_, user)

    up, down = at(xh, (z + 1) % NZ, core), at(xh, (z + 7) % NZ, core)
    across, pair = at(1 - xh, z, core), at(xh, z, 1 - core)

    def owner_at(d):
        return (hist, ((xl + d // NY) % 2) * NY + (y + d % NY) % NY)

    def asker_at(d):
        return (hist, ((xl + d // NY) % 2) * NY + (y + NY - d % NY) % NY)

    def remote(src, dst, send, recv, device):
        return pltpu.make_async_remote_copy(
            src_ref=src, dst_ref=dst, send_sem=send, recv_sem=recv, device_id=device, device_id_type=MESH
        )

    load_length = pltpu.make_async_copy(length_hbm, length_ref, local_sem.at[6])
    load_length.start()
    load_count = pltpu.make_async_copy(count_hbm, count_ref, local_sem.at[7])
    load_count.start()
    load_cache = pltpu.make_async_copy(cache, cache_v, local_sem.at[0])
    load_cache.start()
    load_proj = pltpu.make_async_copy(proj_hbm, proj, local_sem.at[4])
    load_proj.start()
    load_mask = pltpu.make_async_copy(bmask_hbm, bmask, local_sem.at[5])
    load_mask.start()
    load_w = pltpu.make_async_copy(w_out, w_v, local_sem.at[1])
    load_w.start()

    barrier = pltpu.get_barrier_semaphore()
    for d in range(1, PEERS):
        pl.semaphore_signal(barrier, inc=1, device_id=asker_at(d), device_id_type=MESH)
    for device in (up, down, across, pair):
        pl.semaphore_signal(barrier, inc=1, device_id=device, device_id_type=MESH)

    row = lax.broadcasted_iota(jnp.int32, (16, 128), 0)
    lane = lax.broadcasted_iota(jnp.int32, (16, 128), 1)
    zero = jnp.zeros((16, 128), jnp.int32)
    owners, owners_across, want = zero, zero - 1, zero
    for r in range(16):
        owners = jnp.where(row == r, owner_ref[0, r], owners)
        owners_across = jnp.where(lane == r, owner_ref[0, r], owners_across)
        want = jnp.where(row == r, page_ref[0, r], want)
    same = (owners == owners_across) & (lane < row)
    rank = jnp.minimum(jnp.sum(same.astype(jnp.int32), axis=1, keepdims=True), CAP - 1)
    place = (((owners >> 2) ^ xl) & 1) * NY + ((owners - y) & 3)
    turn = zero
    for n in range(1, PEERS):
        turn = jnp.where(place == ORDER[n], n, turn)
    slot = jnp.broadcast_to(rank, (16, 128)) * PEERS + turn
    match = slot == lane
    load_length.wait()
    valid = jnp.clip(length_ref[0] - (hist * 2 + (row >> 3)) * BLK, 0, BLK)

    def pick(values):
        return jnp.sum(jnp.where(match, values, zero), axis=0, keepdims=True)

    r8 = lax.broadcasted_iota(jnp.int32, (8, 128), 0)
    wanted = jnp.clip(pick(want), 0, PAGES - 1)
    heads = jnp.clip(pick(row & 7), 0, H - 1)
    blocks = jnp.clip(pick(row >> 3), 0, 1)
    first = jnp.where(r8 == 0, wanted, jnp.where(r8 == 1, heads, jnp.where(r8 == 2, pick(valid), blocks)))
    msg[0, 0:8, :] = first
    msg[0, 8:24, :] = slot

    pl.semaphore_wait(barrier, PEERS - 1 + 4)

    ask = []
    for d in range(1, PEERS):
        ask.append(remote(msg.at[0, 0:8], asked.at[d], req_send.at[d], req_recv.at[d], owner_at(d)))
    for copy in ask:
        copy.start()
    tell = remote(msg.at[0], msg.at[1], info_sem.at[0], info_sem.at[1], pair)
    tell.start()
    load_proj.wait()
    for e in range(H):
        q = silu(proj[:, 2 * D + e * DH : 2 * D + (e + 1) * DH].astype(jnp.float32))
        queries[z, xh, e] = q.astype(jnp.bfloat16)

    ag_x = remote(queries.at[z, xh], queries.at[z, xh], ag_send.at[0, 4], ag_recv.at[0, 4], across)
    ag_x.start()
    for copy in ask:
        copy.wait_recv()
    copy_asked = pltpu.make_async_copy(asked.at[pl.ds(1, PEERS - 1)], asked_s.at[pl.ds(1, PEERS - 1)], local_sem.at[2])
    copy_asked.start()
    load_cache.wait()
    copy_asked.wait()

    def page_copy(i, d):
        return remote(stage.at[i], pages.at[0, i], page_send.at[i], page_recv.at[i], asker_at(d))

    def serve(k, carry):
        for n in range(1, PEERS):
            i, d = k * PEERS + n, ORDER[n]
            stage[i] = cache_v[asked_s[d, 0, i]]
            page_copy(i, d).start()
        return carry

    lax.fori_loop(0, CAP, serve, 0)
    tell.wait()
    copy_msg = pltpu.make_async_copy(msg, msg_s, local_sem.at[3])
    copy_msg.start()

    ag_x.wait()

    def gather_step(s):
        zu, zd = (z + NZ - s) % NZ, (z + s) % NZ
        if s < 3:
            up_part, down_part = queries.at[zu], queries.at[zd]
        else:
            up_part, down_part = queries.at[zu, 0], queries.at[zd, 1]
        return (
            remote(up_part, up_part, ag_send.at[0, s], ag_recv.at[0, s], up),
            remote(down_part, down_part, ag_send.at[1, s], ag_recv.at[1, s], down),
        )

    steps = [gather_step(s) for s in range(4)]
    for copy in steps[0]:
        copy.start()

    gating[...] = silu(proj[:, 0:D].astype(jnp.float32))
    for e in range(H):
        cols = slice(e * DH, (e + 1) * DH)
        v = silu(proj[:, D + e * DH : D + (e + 1) * DH].astype(jnp.float32)).astype(jnp.bfloat16)
        k = silu(proj[:, 3 * D + e * DH : 3 * D + (e + 1) * DH].astype(jnp.float32)).astype(jnp.bfloat16)
        q = queries[z, xh, e]
        score = jnp.sum(q.astype(jnp.float32) * k.astype(jnp.float32), axis=1, keepdims=True) * SCALE
        own_term[:, cols] = silu(score) * v.astype(jnp.float32)

    load_mask.wait()

    def see(n, carry):
        zd, xd = n // 2, n % 2
        for side in range(2):
            for b in range(2):
                other = core if side == 0 else 1 - core
                m = bmask[xd * 16 + zd * 2 + core, (hist - core + other) * 2 + b].astype(jnp.float32)
                seen[side, b, pl.ds(pl.multiple_of(n * TILE, TILE), TILE), :] = jnp.full((TILE, DH), m, jnp.float32)
        return carry

    lax.fori_loop(0, 2 * NZ, see, 0)
    copy_msg.wait()
    for k in range(CAP):
        pages[0, k * PEERS] = cache_v[msg_s[0, 0, k * PEERS]]

    for s in range(4):
        for direction in range(2):
            steps[s][direction].wait_recv()
            if s < 3:
                steps[s + 1][direction].start()

    def pair_copy(i):
        return remote(pages.at[0, i], pages.at[1, i], pair_send.at[i], pair_recv.at[i], pair)

    rows = lax.broadcasted_iota(jnp.int32, (BLK, DH), 0)
    chunk = 512

    def attend(t, carry):
        side = t % 2
        i = t // 2 - side * LAG

        @pl.when((i >= 0) & (i < SLOTS))
        def _():
            @pl.when((side == 0) & (i % PEERS != 0))
            def _():
                page_copy(i, 1).wait_recv()

            @pl.when(side == 0)
            def _():
                pair_copy(i).start()

            @pl.when(side == 1)
            def _():
                pair_copy(i).wait_recv()

            head = msg_s[side, 1, i]
            live = msg_s[side, 2, i]
            block = msg_s[side, 3, i]
            k = pages[side, i, :, 0:DH]
            v = pages[side, i, :, DH : 2 * DH]
            v = jnp.where(rows < live, v, jnp.zeros_like(v))
            n = chunk // 128
            for j in range(1024 // chunk):
                q = queries[j * n : (j + 1) * n, :, head].reshape(chunk, DH)
                score = lax.dot_general(q, k, (((1,), (1,)), ((), ())), preferred_element_type=jnp.float32)
                half = score * (SCALE * 0.5)
                weight = (half * jnp.tanh(half) + half).astype(jnp.bfloat16)
                term = jnp.dot(weight, v, preferred_element_type=jnp.float32)
                span = slice(j * chunk, (j + 1) * chunk)
                partial[side, i, span, :] = (term * seen[side, block, span, :]).astype(jnp.bfloat16)

        return carry

    lax.fori_loop(0, 2 * (SLOTS + LAG), attend, 0)

    def term_of(zd, xd, e):
        total = None
        for side in range(2):
            for b in range(2):
                part = partial[side, msg_s[side, 8 + b * H + e, 0], pl.ds(pl.multiple_of(zd * 128 + xd * 64, 64), TILE), :]
                part = part.astype(jnp.float32)
                total = part if total is None else total + part
        return total

    def offset_of(g, s):
        return 4 - s if g == 0 else 4 + s

    def heads_of(g, s):
        return range(4) if s else range(2 * g, 2 * g + 2)

    def za_copy(g, s, j):
        part = pl.ds(heads_of(g, s)[0], len(heads_of(g, s)))
        return remote(
            za_send.at[g, s, j, part], za_recv.at[g, s, j, part], za_ssem.at[g, s, j], za_rsem.at[g, s, j], (up, down)[g]
        )

    def zb_copy(g, s):
        part = pl.ds(heads_of(g, s)[0], len(heads_of(g, s)))
        return remote(zb_send.at[g, s, part], zb_recv.at[g, s, part], zb_ssem.at[g, s], zb_rsem.at[g, s], (up, down)[g])

    def xb_copy(o):
        return remote(xb_send.at[o], xb_recv.at[o], xb_ssem.at[o], xb_rsem.at[o], across)

    def a_step(s):
        for j in range(2):
            for g in range(2):
                zd = (z + offset_of(g, s)) % NZ
                if s:
                    za_copy(g, s - 1, j).wait_recv()
                for e in heads_of(g, s):
                    v = term_of(zd, j, e)
                    if s and e in heads_of(g, s - 1):
                        v = v + za_recv[g, s - 1, j, e].astype(jnp.float32)
                    za_send[g, s, j, e] = v.astype(jnp.bfloat16)
                za_copy(g, s, j).start()

    def x_step(o):
        for e in range(4):
            xb_send[o, e] = term_of((z + o) % NZ, 1 - xh, 4 + e).astype(jnp.bfloat16)
        xb_copy(o).start()

    def b_step(s):
        for g in range(2):
            o = offset_of(g, s)
            if s or g == 0:
                xb_copy(o).wait_recv()
            if s:
                zb_copy(g, s - 1).wait_recv()
            for e in heads_of(g, s):
                v = term_of((z + o) % NZ, xh, 4 + e) + xb_recv[o, e].astype(jnp.float32)
                if s and e in heads_of(g, s - 1):
                    v = v + zb_recv[g, s - 1, e].astype(jnp.float32)
                zb_send[g, s, e] = v.astype(jnp.bfloat16)
            zb_copy(g, s).start()

    x_step(4)
    a_step(0)
    x_step(3)
    x_step(5)
    x_step(2)
    x_step(6)
    a_step(1)
    b_step(0)
    x_step(1)
    x_step(7)
    x_step(0)
    a_step(2)
    b_step(1)
    a_step(3)
    b_step(2)

    def a_final(xd, e):
        v = term_of(z, xd, e) + za_recv[0, 3, xd, e].astype(jnp.float32)
        return v + za_recv[1, 3, xd, e].astype(jnp.float32)

    for j in range(2):
        for g in range(2):
            za_copy(g, 3, j).wait_recv()
    for e in range(4):
        xa_send[e] = a_final(1 - xh, e).astype(jnp.bfloat16)
    xa_copy = remote(xa_send, xa_recv, xa_sem.at[0], xa_sem.at[1], across)
    xa_copy.start()
    b_step(3)
    for e in range(4):
        cols = slice(e * DH, (e + 1) * DH)
        own_term[:, cols] = own_term[:, cols] + a_final(xh, e)
    load_w.wait()
    load_count.wait()
    xa_copy.wait()
    for e in range(4):
        cols = slice(e * DH, (e + 1) * DH)
        own_term[:, cols] = own_term[:, cols] + xa_recv[e].astype(jnp.float32)
    xb_copy(0).wait_recv()
    for g in range(2):
        zb_copy(g, 3).wait_recv()
    for e in range(4):
        cols = slice((4 + e) * DH, (5 + e) * DH)
        v = term_of(z, xh, 4 + e) + xb_recv[0, e].astype(jnp.float32)
        v = v + zb_recv[0, 3, e].astype(jnp.float32) + zb_recv[1, 3, e].astype(jnp.float32)
        own_term[:, cols] = own_term[:, cols] + v
    attn = own_term[...]
    centre = attn - jnp.mean(attn, axis=1, keepdims=True)
    variance = jnp.mean(centre * centre, axis=1, keepdims=True)
    mixed = (centre * lax.rsqrt(variance + 1e-05) * gain[...] * gating[...]).astype(jnp.bfloat16)
    out = jnp.dot(mixed, w_v[...], preferred_element_type=jnp.float32)
    live_row = hist * TILE + lax.broadcasted_iota(jnp.int32, (TILE, D), 0) < count_ref[0]
    result[...] = jnp.where(live_row, out, jnp.zeros_like(out)).astype(jnp.bfloat16)

    for copy in ask:
        copy.wait_send()
    for s in range(4):
        for direction in range(2):
            steps[s][direction].wait_send()

    def drain_pages(k, carry):
        for n in range(PEERS):
            if n:
                page_copy(k * PEERS + n, ORDER[n]).wait_send()
            pair_copy(k * PEERS + n).wait_send()
        return carry

    lax.fori_loop(0, CAP, drain_pages, 0)

    for s in range(4):
        for g in range(2):
            for j in range(2):
                za_copy(g, s, j).wait_send()
            zb_copy(g, s).wait_send()
    for o in range(NZ):
        xb_copy(o).wait_send()


def body(proj, cache, owner, page, length, count, bmask, gain, w_out):
    vmem, smem = pl.BlockSpec(memory_space=pltpu.VMEM), pl.BlockSpec(memory_space=pltpu.SMEM)
    anywhere = pl.BlockSpec(memory_space=pl.ANY)
    dma = pltpu.SemaphoreType.DMA
    bf, f32, i32 = jnp.bfloat16, jnp.float32, jnp.int32
    out = pl.pallas_call(
        kernel,
        out_shape=jax.ShapeDtypeStruct((TILE, D), bf),
        in_specs=[anywhere, anywhere, smem, smem, vmem, anywhere, anywhere, anywhere, anywhere],
        out_specs=vmem,
        scratch_shapes=[
            pltpu.SMEM((1,), i32),
            pltpu.SMEM((1,), i32),
            pltpu.SMEM((32, 64), i32),
            pltpu.VMEM((2, 2, 1024, DH), f32),
            pltpu.VMEM((TILE, 4 * D), bf),
            pltpu.VMEM((16, BLK, 2 * DH), bf),
            pltpu.VMEM((D, D), bf),
            pltpu.VMEM((SLOTS, BLK, 2 * DH), bf),
            pltpu.VMEM((2, SLOTS, BLK, 2 * DH), bf),
            pltpu.VMEM((NZ, 2, H, TILE, DH), bf),
            pltpu.VMEM((2, SLOTS, 1024, DH), bf),
            pltpu.VMEM((TILE, D), f32),
            pltpu.VMEM((TILE, D), f32),
            pltpu.VMEM((2, 24, 128), i32),
            pltpu.VMEM((PEERS, 8, 128), i32),
            pltpu.SMEM((2, 24, 128), i32),
            pltpu.SMEM((PEERS, 8, 128), i32),
            pltpu.VMEM((2, 4, 2, 4, TILE, DH), bf),
            pltpu.VMEM((2, 4, 2, 4, TILE, DH), bf),
            pltpu.VMEM((2, 4, 4, TILE, DH), bf),
            pltpu.VMEM((2, 4, 4, TILE, DH), bf),
            pltpu.VMEM((NZ, 4, TILE, DH), bf),
            pltpu.VMEM((NZ, 4, TILE, DH), bf),
            pltpu.VMEM((4, TILE, DH), bf),
            pltpu.VMEM((4, TILE, DH), bf),
            dma((8,)),
            dma((PEERS,)),
            dma((PEERS,)),
            dma((SLOTS,)),
            dma((SLOTS,)),
            dma((SLOTS,)),
            dma((SLOTS,)),
            dma((2,)),
            dma((2, 5)),
            dma((2, 5)),
            dma((2, 4, 2)),
            dma((2, 4, 2)),
            dma((2, 4)),
            dma((2, 4)),
            dma((NZ,)),
            dma((NZ,)),
            dma((2,)),
        ],
        compiler_params=pltpu.CompilerParams(
            collective_id=0, has_side_effects=True, vmem_limit_bytes=60 * 1024 * 1024
        ),
        name="score_candidates",
    )(length, count, owner.reshape(1, 16), page, gain.reshape(1, D), bmask[0], proj[0], cache[0], w_out)
    return out[None]


def solution(mesh):
    return jax.shard_map(
        body,
        mesh=mesh,
        in_specs=(
            P("user", "hist", None),
            P("hist", "user", None, None),
            P("user", "hist", None),
            P("user", "hist"),
            P("user"),
            P("user"),
            P("user", None, None),
            P(),
            P(),
        ),
        out_specs=P("user", "hist", None),
        check_vma=False,
    )
```

```python
import jax
import jax.numpy as jnp
from jax import lax
from jax.experimental import pallas as pl
from jax.experimental.pallas import tpu as pltpu
from jax.sharding import PartitionSpec as P

D = 1024
H = 8
DH = 128
BLK = 512
TILE = 64
NY = 4
NZ = 8
PEERS = 8
CAP = 3
PAGES = 16
SLOTS = PEERS * CAP
LAG = 1
ORDER = (0, 7, 1, 5, 3, 4, 2, 6)
SCALE = DH ** (-0.5)
MESH = pl.DeviceIdType.MESH


def silu(v):
    half = v * 0.5
    return half * jnp.tanh(half) + half


def kernel(
    length_hbm,
    count_hbm,
    owner_ref,
    page_ref,
    gain,
    bmask_hbm,
    proj_hbm,
    cache,
    w_out,
    result,
    length_ref,
    count_ref,
    bmask,
    seen,
    proj,
    cache_v,
    w_v,
    stage,
    pages,
    queries,
    partial,
    gating,
    own_term,
    msg,
    asked,
    msg_s,
    asked_s,
    za_send,
    za_recv,
    zb_send,
    zb_recv,
    xb_send,
    xb_recv,
    xa_send,
    xa_recv,
    local_sem,
    req_send,
    req_recv,
    page_send,
    page_recv,
    pair_send,
    pair_recv,
    info_sem,
    ag_send,
    ag_recv,
    za_ssem,
    za_rsem,
    zb_ssem,
    zb_rsem,
    xb_ssem,
    xb_rsem,
    xa_sem,
):
    hist, user = lax.axis_index("hist"), lax.axis_index("user")
    xh, z, core = hist // 16, (hist // 2) % NZ, hist % 2
    xl, y = user // NY, user % NY

    def at(xh_, z_, core_):
        return (xh_ * 16 + z_ * 2 + core_, user)

    up, down = at(xh, (z + 1) % NZ, core), at(xh, (z + 7) % NZ, core)
    across, pair = at(1 - xh, z, core), at(xh, z, 1 - core)

    def owner_at(d):
        return (hist, ((xl + d // NY) % 2) * NY + (y + d % NY) % NY)

    def asker_at(d):
        return (hist, ((xl + d // NY) % 2) * NY + (y + NY - d % NY) % NY)

    def remote(src, dst, send, recv, device):
        return pltpu.make_async_remote_copy(
            src_ref=src, dst_ref=dst, send_sem=send, recv_sem=recv, device_id=device, device_id_type=MESH
        )

    load_length = pltpu.make_async_copy(length_hbm, length_ref, local_sem.at[6])
    load_length.start()
    load_count = pltpu.make_async_copy(count_hbm, count_ref, local_sem.at[7])
    load_count.start()
    load_cache = pltpu.make_async_copy(cache, cache_v, local_sem.at[0])
    load_cache.start()
    load_proj = pltpu.make_async_copy(proj_hbm, proj, local_sem.at[4])
    load_proj.start()
    load_mask = pltpu.make_async_copy(bmask_hbm, bmask, local_sem.at[5])
    load_mask.start()
    load_w = pltpu.make_async_copy(w_out, w_v, local_sem.at[1])
    load_w.start()

    barrier = pltpu.get_barrier_semaphore()
    for d in range(1, PEERS):
        pl.semaphore_signal(barrier, inc=1, device_id=asker_at(d), device_id_type=MESH)
    for device in (up, down, across, pair):
        pl.semaphore_signal(barrier, inc=1, device_id=device, device_id_type=MESH)

    row = lax.broadcasted_iota(jnp.int32, (16, 128), 0)
    lane = lax.broadcasted_iota(jnp.int32, (16, 128), 1)
    zero = jnp.zeros((16, 128), jnp.int32)
    owners, owners_across, want = zero, zero - 1, zero
    for r in range(16):
        owners = jnp.where(row == r, owner_ref[0, r], owners)
        owners_across = jnp.where(lane == r, owner_ref[0, r], owners_across)
        want = jnp.where(row == r, page_ref[0, r], want)
    same = (owners == owners_across) & (lane < row)
    rank = jnp.minimum(jnp.sum(same.astype(jnp.int32), axis=1, keepdims=True), CAP - 1)
    place = (((owners >> 2) ^ xl) & 1) * NY + ((owners - y) & 3)
    turn = zero
    for n in range(1, PEERS):
        turn = jnp.where(place == ORDER[n], n, turn)
    slot = jnp.broadcast_to(rank, (16, 128)) * PEERS + turn
    match = slot == lane
    load_length.wait()
    valid = jnp.clip(length_ref[0] - (hist * 2 + (row >> 3)) * BLK, 0, BLK)

    def pick(values):
        return jnp.sum(jnp.where(match, values, zero), axis=0, keepdims=True)

    r8 = lax.broadcasted_iota(jnp.int32, (8, 128), 0)
    wanted = jnp.clip(pick(want), 0, PAGES - 1)
    heads = jnp.clip(pick(row & 7), 0, H - 1)
    blocks = jnp.clip(pick(row >> 3), 0, 1)
    first = jnp.where(r8 == 0, wanted, jnp.where(r8 == 1, heads, jnp.where(r8 == 2, pick(valid), blocks)))
    msg[0, 0:8, :] = first
    msg[0, 8:24, :] = slot

    pl.semaphore_wait(barrier, PEERS - 1 + 4)

    ask = []
    for d in range(1, PEERS):
        ask.append(remote(msg.at[0, 0:8], asked.at[d], req_send.at[d], req_recv.at[d], owner_at(d)))
    for copy in ask:
        copy.start()
    tell = remote(msg.at[0], msg.at[1], info_sem.at[0], info_sem.at[1], pair)
    tell.start()
    load_proj.wait()
    for e in range(H):
        q = silu(proj[:, 2 * D + e * DH : 2 * D + (e + 1) * DH].astype(jnp.float32))
        queries[z, xh, e] = q.astype(jnp.bfloat16)

    ag_x = remote(queries.at[z, xh], queries.at[z, xh], ag_send.at[0, 4], ag_recv.at[0, 4], across)
    ag_x.start()
    for copy in ask:
        copy.wait_recv()
    copy_asked = pltpu.make_async_copy(asked.at[pl.ds(1, PEERS - 1)], asked_s.at[pl.ds(1, PEERS - 1)], local_sem.at[2])
    copy_asked.start()
    load_cache.wait()
    copy_asked.wait()

    def page_copy(i, d):
        return remote(stage.at[i], pages.at[0, i], page_send.at[i], page_recv.at[i], asker_at(d))

    def serve(k, carry):
        for n in range(1, PEERS):
            i, d = k * PEERS + n, ORDER[n]
            stage[i] = cache_v[asked_s[d, 0, i]]
            page_copy(i, d).start()
        return carry

    lax.fori_loop(0, CAP, serve, 0)
    tell.wait()
    copy_msg = pltpu.make_async_copy(msg, msg_s, local_sem.at[3])
    copy_msg.start()

    ag_x.wait()

    def gather_step(s):
        zu, zd = (z + NZ - s) % NZ, (z + s) % NZ
        if s < 3:
            up_part, down_part = queries.at[zu], queries.at[zd]
        else:
            up_part, down_part = queries.at[zu, 0], queries.at[zd, 1]
        return (
            remote(up_part, up_part, ag_send.at[0, s], ag_recv.at[0, s], up),
            remote(down_part, down_part, ag_send.at[1, s], ag_recv.at[1, s], down),
        )

    steps = [gather_step(s) for s in range(4)]
    for copy in steps[0]:
        copy.start()

    gating[...] = silu(proj[:, 0:D].astype(jnp.float32))
    for e in range(H):
        cols = slice(e * DH, (e + 1) * DH)
        v = silu(proj[:, D + e * DH : D + (e + 1) * DH].astype(jnp.float32)).astype(jnp.bfloat16)
        k = silu(proj[:, 3 * D + e * DH : 3 * D + (e + 1) * DH].astype(jnp.float32)).astype(jnp.bfloat16)
        q = queries[z, xh, e]
        score = jnp.sum(q.astype(jnp.float32) * k.astype(jnp.float32), axis=1, keepdims=True) * SCALE
        own_term[:, cols] = silu(score) * v.astype(jnp.float32)

    load_mask.wait()

    def see(n, carry):
        zd, xd = n // 2, n % 2
        for side in range(2):
            for b in range(2):
                other = core if side == 0 else 1 - core
                m = bmask[xd * 16 + zd * 2 + core, (hist - core + other) * 2 + b].astype(jnp.float32)
                seen[side, b, pl.ds(pl.multiple_of(n * TILE, TILE), TILE), :] = jnp.full((TILE, DH), m, jnp.float32)
        return carry

    lax.fori_loop(0, 2 * NZ, see, 0)
    copy_msg.wait()
    for k in range(CAP):
        pages[0, k * PEERS] = cache_v[msg_s[0, 0, k * PEERS]]

    for s in range(4):
        for direction in range(2):
            steps[s][direction].wait_recv()
            if s < 3:
                steps[s + 1][direction].start()

    def pair_copy(i):
        return remote(pages.at[0, i], pages.at[1, i], pair_send.at[i], pair_recv.at[i], pair)

    rows = lax.broadcasted_iota(jnp.int32, (BLK, DH), 0)
    chunk = 512

    def attend(t, carry):
        side = t % 2
        i = t // 2 - side * LAG

        @pl.when((i >= 0) & (i < SLOTS))
        def _():
            @pl.when((side == 0) & (i % PEERS != 0))
            def _():
                page_copy(i, 1).wait_recv()

            @pl.when(side == 0)
            def _():
                pair_copy(i).start()

            @pl.when(side == 1)
            def _():
                pair_copy(i).wait_recv()

            head = msg_s[side, 1, i]
            live = msg_s[side, 2, i]
            block = msg_s[side, 3, i]
            k = pages[side, i, :, 0:DH]
            v = pages[side, i, :, DH : 2 * DH]
            v = jnp.where(rows < live, v, jnp.zeros_like(v))
            n = chunk // 128
            for j in range(1024 // chunk):
                q = queries[j * n : (j + 1) * n, :, head].reshape(chunk, DH)
                score = lax.dot_general(q, k, (((1,), (1,)), ((), ())), preferred_element_type=jnp.float32)
                half = score * (SCALE * 0.5)
                weight = (half * jnp.tanh(half) + half).astype(jnp.bfloat16)
                term = jnp.dot(weight, v, preferred_element_type=jnp.float32)
                span = slice(j * chunk, (j + 1) * chunk)
                partial[side, i, span, :] = (term * seen[side, block, span, :]).astype(jnp.bfloat16)

        return carry

    lax.fori_loop(0, 2 * (SLOTS + LAG), attend, 0)

    def term_of(zd, xd, e):
        total = None
        for side in range(2):
            for b in range(2):
                part = partial[side, msg_s[side, 8 + b * H + e, 0], pl.ds(pl.multiple_of(zd * 128 + xd * 64, 64), TILE), :]
                part = part.astype(jnp.float32)
                total = part if total is None else total + part
        return total

    def offset_of(g, s):
        return 4 - s if g == 0 else 4 + s

    def heads_of(g, s):
        return range(4) if s else range(2 * g, 2 * g + 2)

    def za_copy(g, s, j):
        part = pl.ds(heads_of(g, s)[0], len(heads_of(g, s)))
        return remote(
            za_send.at[g, s, j, part], za_recv.at[g, s, j, part], za_ssem.at[g, s, j], za_rsem.at[g, s, j], (up, down)[g]
        )

    def zb_copy(g, s):
        part = pl.ds(heads_of(g, s)[0], len(heads_of(g, s)))
        return remote(zb_send.at[g, s, part], zb_recv.at[g, s, part], zb_ssem.at[g, s], zb_rsem.at[g, s], (up, down)[g])

    def xb_copy(o):
        return remote(xb_send.at[o], xb_recv.at[o], xb_ssem.at[o], xb_rsem.at[o], across)

    def a_step(s):
        for j in range(2):
            for g in range(2):
                zd = (z + offset_of(g, s)) % NZ
                if s:
                    za_copy(g, s - 1, j).wait_recv()
                for e in heads_of(g, s):
                    v = term_of(zd, j, e)
                    if s and e in heads_of(g, s - 1):
                        v = v + za_recv[g, s - 1, j, e].astype(jnp.float32)
                    za_send[g, s, j, e] = v.astype(jnp.bfloat16)
                za_copy(g, s, j).start()

    def x_step(o):
        for e in range(4):
            xb_send[o, e] = term_of((z + o) % NZ, 1 - xh, 4 + e).astype(jnp.bfloat16)
        xb_copy(o).start()

    def b_step(s):
        for g in range(2):
            o = offset_of(g, s)
            if s or g == 0:
                xb_copy(o).wait_recv()
            if s:
                zb_copy(g, s - 1).wait_recv()
            for e in heads_of(g, s):
                v = term_of((z + o) % NZ, xh, 4 + e) + xb_recv[o, e].astype(jnp.float32)
                if s and e in heads_of(g, s - 1):
                    v = v + zb_recv[g, s - 1, e].astype(jnp.float32)
                zb_send[g, s, e] = v.astype(jnp.bfloat16)
            zb_copy(g, s).start()

    x_step(4)
    a_step(0)
    x_step(3)
    x_step(5)
    x_step(2)
    x_step(6)
    a_step(1)
    b_step(0)
    x_step(1)
    x_step(7)
    x_step(0)
    a_step(2)
    b_step(1)
    a_step(3)
    b_step(2)

    def a_final(xd, e):
        v = term_of(z, xd, e) + za_recv[0, 3, xd, e].astype(jnp.float32)
        return v + za_recv[1, 3, xd, e].astype(jnp.float32)

    for j in range(2):
        for g in range(2):
            za_copy(g, 3, j).wait_recv()
    for e in range(4):
        xa_send[e] = a_final(1 - xh, e).astype(jnp.bfloat16)
    xa_copy = remote(xa_send, xa_recv, xa_sem.at[0], xa_sem.at[1], across)
    xa_copy.start()
    b_step(3)
    for e in range(4):
        cols = slice(e * DH, (e + 1) * DH)
        own_term[:, cols] = own_term[:, cols] + a_final(xh, e)
    load_w.wait()
    load_count.wait()
    xa_copy.wait()
    for e in range(4):
        cols = slice(e * DH, (e + 1) * DH)
        own_term[:, cols] = own_term[:, cols] + xa_recv[e].astype(jnp.float32)
    xb_copy(0).wait_recv()
    for g in range(2):
        zb_copy(g, 3).wait_recv()
    for e in range(4):
        cols = slice((4 + e) * DH, (5 + e) * DH)
        v = term_of(z, xh, 4 + e) + xb_recv[0, e].astype(jnp.float32)
        v = v + zb_recv[0, 3, e].astype(jnp.float32) + zb_recv[1, 3, e].astype(jnp.float32)
        own_term[:, cols] = own_term[:, cols] + v
    attn = own_term[...]
    centre = attn - jnp.mean(attn, axis=1, keepdims=True)
    variance = jnp.mean(centre * centre, axis=1, keepdims=True)
    mixed = (centre * lax.rsqrt(variance + 1e-05) * gain[...] * gating[...]).astype(jnp.bfloat16)
    out = jnp.dot(mixed, w_v[...], preferred_element_type=jnp.float32)
    live_row = hist * TILE + lax.broadcasted_iota(jnp.int32, (TILE, D), 0) < count_ref[0]
    result[...] = jnp.where(live_row, out, jnp.zeros_like(out)).astype(jnp.bfloat16)

    for copy in ask:
        copy.wait_send()
    for s in range(4):
        for direction in range(2):
            steps[s][direction].wait_send()

    def drain_pages(k, carry):
        for n in range(PEERS):
            if n:
                page_copy(k * PEERS + n, ORDER[n]).wait_send()
            pair_copy(k * PEERS + n).wait_send()
        return carry

    lax.fori_loop(0, CAP, drain_pages, 0)

    for s in range(4):
        for g in range(2):
            for j in range(2):
                za_copy(g, s, j).wait_send()
            zb_copy(g, s).wait_send()
    for o in range(NZ):
        xb_copy(o).wait_send()


def body(proj, cache, owner, page, length, count, bmask, gain, w_out):
    vmem, smem = pl.BlockSpec(memory_space=pltpu.VMEM), pl.BlockSpec(memory_space=pltpu.SMEM)
    anywhere = pl.BlockSpec(memory_space=pl.ANY)
    dma = pltpu.SemaphoreType.DMA
    bf, f32, i32 = jnp.bfloat16, jnp.float32, jnp.int32
    out = pl.pallas_call(
        kernel,
        out_shape=jax.ShapeDtypeStruct((TILE, D), bf),
        in_specs=[anywhere, anywhere, smem, smem, vmem, anywhere, anywhere, anywhere, anywhere],
        out_specs=vmem,
        scratch_shapes=[
            pltpu.SMEM((1,), i32),
            pltpu.SMEM((1,), i32),
            pltpu.SMEM((32, 64), i32),
            pltpu.VMEM((2, 2, 1024, DH), f32),
            pltpu.VMEM((TILE, 4 * D), bf),
            pltpu.VMEM((16, BLK, 2 * DH), bf),
            pltpu.VMEM((D, D), bf),
            pltpu.VMEM((SLOTS, BLK, 2 * DH), bf),
            pltpu.VMEM((2, SLOTS, BLK, 2 * DH), bf),
            pltpu.VMEM((NZ, 2, H, TILE, DH), bf),
            pltpu.VMEM((2, SLOTS, 1024, DH), bf),
            pltpu.VMEM((TILE, D), f32),
            pltpu.VMEM((TILE, D), f32),
            pltpu.VMEM((2, 24, 128), i32),
            pltpu.VMEM((PEERS, 8, 128), i32),
            pltpu.SMEM((2, 24, 128), i32),
            pltpu.SMEM((PEERS, 8, 128), i32),
            pltpu.VMEM((2, 4, 2, 4, TILE, DH), bf),
            pltpu.VMEM((2, 4, 2, 4, TILE, DH), bf),
            pltpu.VMEM((2, 4, 4, TILE, DH), bf),
            pltpu.VMEM((2, 4, 4, TILE, DH), bf),
            pltpu.VMEM((NZ, 4, TILE, DH), bf),
            pltpu.VMEM((NZ, 4, TILE, DH), bf),
            pltpu.VMEM((4, TILE, DH), bf),
            pltpu.VMEM((4, TILE, DH), bf),
            dma((8,)),
            dma((PEERS,)),
            dma((PEERS,)),
            dma((SLOTS,)),
            dma((SLOTS,)),
            dma((SLOTS,)),
            dma((SLOTS,)),
            dma((2,)),
            dma((2, 5)),
            dma((2, 5)),
            dma((2, 4, 2)),
            dma((2, 4, 2)),
            dma((2, 4)),
            dma((2, 4)),
            dma((NZ,)),
            dma((NZ,)),
            dma((2,)),
        ],
        compiler_params=pltpu.CompilerParams(
            collective_id=0, has_side_effects=True, vmem_limit_bytes=60 * 1024 * 1024
        ),
        name="score_candidates",
    )(length, count, owner.reshape(1, 16), page, gain.reshape(1, D), bmask[0], proj[0], cache[0], w_out)
    return out[None]


def solution(mesh):
    return jax.shard_map(
        body,
        mesh=mesh,
        in_specs=(
            P("user", "hist", None),
            P("hist", "user", None, None),
            P("user", "hist", None),
            P("user", "hist"),
            P("user"),
            P("user"),
            P("user", None, None),
            P(),
            P(),
        ),
        out_specs=P("user", "hist", None),
        check_vma=False,
    )
```
